512 devices in a mesh: stn: 64 (over y_hi, z, core), blk: 8 (over y_lo, x).
Axes of the slice: x: 4, y: 4 (y_hi: 2, y_lo: 2; y = y_hi * 2 + y_lo), z: 16, core: 2. Of those that a mesh axis runs over, the one named last changes fastest.
Arguments:
- samples: int32 [2, 512, 262144], P(None, 'stn', 'blk'), may hold values from -128 to 127, as said below
- fir_taps: float32 [8, 1024], replicated, may hold values from -2 to 2
- station_order: int32 [512], replicated, may hold values from 0 to 511, each once
Outputs:
- coherence: bfloat16 [2, 1024, 512, 512], P(None, 'stn', 'blk')
The draws below stay inside these ranges and needn't reach their ends.
Inputs may be any that keep to these rules, and one draw needn't show every extreme that they name: `samples`: quantized voltages, real parts in row 0 and imaginary parts in row 1 of the leading dimension. `station_order`: each station number appears exactly once.
All inputs are finite; a program needn't handle non-finite values.
Results may differ from the reference program's by a relative error of at most 0.0033.
Values may be sent and summed in bfloat16 or wider, within the bound.
A program may use at most 64 MiB of HBM per device.

```python
import math
import jax
import jax.numpy as jnp
from jax import lax

STATIONS = 512
CHANNELS = 1024
TAPS = 8
SPECTRA = 256


source_count = 8


def draw_samples(key, part):
    gain_key = jax.random.fold_in(key, 101)
    signal_key = jax.random.fold_in(key, 202)
    noise_key = jax.random.fold_in(key, 303)
    level_key = jax.random.fold_in(key, 404)
    station_gain = jax.random.randint(gain_key, (STATIONS, source_count), -2, 3)
    signals = jax.random.randint(signal_key, (2, source_count, SPECTRA * CHANNELS), -8, 9)
    noise_level = jax.random.randint(level_key, (STATIONS, 1), 1, 5)
    noise_part = jax.random.randint(noise_key, (2, STATIONS, SPECTRA * CHANNELS), -40, 41)
    noise_part = noise_part * noise_level[None, :, :] // 4
    mixture = jnp.einsum('as,pst->pat', station_gain, signals) + noise_part
    return jnp.clip(mixture, -128, 127).astype(jnp.int32)


def noise(key, dims, deviation, reach, kind=jnp.bfloat16):
    return jnp.clip(deviation * jax.random.normal(key, dims, jnp.float32), -reach, reach).astype(kind)


def setup_inputs(seed: int = 0) -> dict:
    arg_keys = jax.random.split(jax.random.key(seed), 4)
    return {
        "samples": draw_samples(jax.random.fold_in(arg_keys[3], 71), 0),
        "fir_taps": noise(arg_keys[1], (TAPS, CHANNELS), TAPS ** -0.5, 2.0, jnp.float32),
        "station_order": jax.random.permutation(arg_keys[2], STATIONS).astype(jnp.int32),
    }


epsilon = 1e-06

def dft_tables(channels):
    channel_index = jnp.arange(channels, dtype=jnp.int32)
    phase_index = channel_index[:, None] * channel_index[None, :] % channels
    angle_table = phase_index.astype(jnp.float32) * (2.0 * math.pi / channels)
    return (jnp.cos(angle_table).astype(jnp.bfloat16), jnp.sin(angle_table).astype(jnp.bfloat16))

def station_spectra(block_samples, fir_taps, cosine_table, sine_table):
    block_width = block_samples.shape[1]
    frames = block_samples.astype(jnp.float32).reshape(2, block_width, SPECTRA, CHANNELS)
    padded = jnp.concatenate([jnp.zeros((2, block_width, TAPS - 1, CHANNELS), jnp.float32), frames], axis=2)
    filtered = fir_taps[0] * padded[:, :, 0:SPECTRA]
    for tap_index in range(1, TAPS):
        filtered = filtered + fir_taps[tap_index] * padded[:, :, tap_index:tap_index + SPECTRA]
    filtered = lax.optimization_barrier(filtered.astype(jnp.bfloat16)).astype(jnp.float32)
    cosine_part = jnp.einsum('kc,pasc->pksa', cosine_table.astype(jnp.float32), filtered, precision=lax.Precision.HIGHEST)
    sine_part = jnp.einsum('kc,pasc->pksa', sine_table.astype(jnp.float32), filtered, precision=lax.Precision.HIGHEST)
    real_part = cosine_part[0] + sine_part[1]
    imag_part = cosine_part[1] - sine_part[0]
    return jnp.stack([real_part, imag_part]).astype(jnp.bfloat16)

def reference(samples, fir_taps, station_order):
    cosine_table, sine_table = dft_tables(CHANNELS)
    block_width = 16

    def one_block(block_index):
        block_samples = lax.dynamic_slice_in_dim(samples, block_index * block_width, block_width, 1)
        return station_spectra(block_samples, fir_taps, cosine_table, sine_table)
    blocks = lax.map(one_block, jnp.arange(STATIONS // block_width, dtype=jnp.int32))
    spectra = jnp.transpose(blocks, (1, 2, 3, 0, 4)).reshape(2, CHANNELS, SPECTRA, STATIONS)
    ordered = jnp.take(spectra, station_order, axis=3)
    group_width = 16

    def one_group(group_index):
        group_data = lax.dynamic_slice_in_dim(ordered, group_index * group_width, group_width, 1).astype(jnp.float32)
        real_vis = jnp.einsum('pksa,pksb->kab', group_data, group_data, precision=lax.Precision.HIGHEST)
        imag_vis = jnp.einsum('ksa,ksb->kab', group_data[1], group_data[0], precision=lax.Precision.HIGHEST) - jnp.einsum('ksa,ksb->kab', group_data[0], group_data[1], precision=lax.Precision.HIGHEST)
        power_sum = lax.optimization_barrier(jnp.sum(group_data * group_data, axis=(0, 2)))
        scale_row = lax.rsqrt(power_sum + epsilon)
        visibility = jnp.stack([real_vis, imag_vis])
        return (visibility * scale_row[None, :, :, None] * scale_row[None, :, None, :]).astype(jnp.bfloat16)
    groups = lax.map(one_group, jnp.arange(CHANNELS // group_width, dtype=jnp.int32))
    return jnp.transpose(groups, (1, 0, 2, 3, 4)).reshape(2, CHANNELS, STATIONS, STATIONS)
```

```python
import functools
import math

import jax
import jax.numpy as jnp
from jax import lax
from jax.experimental import pallas as pl
from jax.experimental.pallas import tpu as pltpu
from jax.sharding import PartitionSpec as P

epsilon = 1e-06
MESH = pl.DeviceIdType.MESH


def passed_along(value, axis, steps):
    count = lax.axis_size(axis)
    initial, last = (max(0, -steps), min(count, count - steps))
    return lax.ppermute(value, axis, [(source, source + steps) for source in range(initial, last)])


def dft_tables(channels):
    channel_index = jnp.arange(channels, dtype=jnp.int32)
    phase_index = channel_index[:, None] * channel_index[None, :] % channels
    angle_table = phase_index.astype(jnp.float32) * (2.0 * math.pi / channels)
    return (jnp.cos(angle_table).astype(jnp.bfloat16), jnp.sin(angle_table).astype(jnp.bfloat16))


def exchange_kernel(axis, count, in_ref, out_ref, send_sem, recv_sem, own_sem):
    me = lax.axis_index(axis)
    barrier = pltpu.get_barrier_semaphore()

    def greet(step, carry):
        pl.semaphore_signal(
            barrier, inc=1, device_id={axis: lax.rem(me + step, count)}, device_id_type=MESH
        )
        return carry

    lax.fori_loop(1, count, greet, 0)
    own = pltpu.make_async_copy(in_ref.at[me], out_ref.at[me], own_sem)
    own.start()
    pl.semaphore_wait(barrier, count - 1)

    def send(step, carry):
        target = lax.rem(me + step, count)
        pltpu.make_async_remote_copy(
            src_ref=in_ref.at[target],
            dst_ref=out_ref.at[me],
            send_sem=send_sem,
            recv_sem=recv_sem,
            device_id={axis: target},
            device_id_type=MESH,
        ).start()
        return carry

    lax.fori_loop(1, count, send, 0)
    others = pl.ds(0, count - 1)
    pltpu.make_async_copy(in_ref.at[others], out_ref.at[others], recv_sem).wait()
    pltpu.make_async_copy(in_ref.at[others], out_ref.at[others], send_sem).wait()
    own.wait()


def exchange(blocks, axis, identity):
    count = lax.axis_size(axis)
    shape = blocks.shape
    flat = blocks.reshape(count, -1, 128)
    flat = pl.pallas_call(
        functools.partial(exchange_kernel, axis, count),
        out_shape=jax.ShapeDtypeStruct(flat.shape, flat.dtype),
        in_specs=[pl.BlockSpec(memory_space=pltpu.VMEM)],
        out_specs=pl.BlockSpec(memory_space=pltpu.VMEM),
        scratch_shapes=[pltpu.SemaphoreType.DMA] * 3,
        compiler_params=pltpu.CompilerParams(
            collective_id=identity, has_side_effects=True, vmem_limit_bytes=32 << 20
        ),
    )(flat)
    return flat.reshape(shape)


def per_device(samples, fir_taps, station_order):
    tap_count = fir_taps.shape[0]
    channels = fir_taps.shape[1]
    stations_local = samples.shape[1]
    spectra_local = samples.shape[2] // channels
    stations = station_order.shape[0]
    groups = lax.axis_size("stn")
    blocks = lax.axis_size("blk")
    per_group = channels // groups
    per_owner = per_group // blocks
    frames = samples.reshape(2, stations_local, spectra_local, channels)
    earlier = frames[:, :, spectra_local - (tap_count - 1) :, :].astype(jnp.bfloat16)
    earlier = passed_along(earlier, "blk", 1)
    extended = jnp.concatenate([earlier.astype(jnp.float32), frames.astype(jnp.float32)], axis=2)
    filtered = fir_taps[0] * extended[:, :, 0:spectra_local]
    for tap_index in range(1, tap_count):
        filtered = (
            filtered + fir_taps[tap_index] * extended[:, :, tap_index : tap_index + spectra_local]
        )
    filtered = filtered.astype(jnp.bfloat16)
    cosine_table, sine_table = dft_tables(channels)
    cosine_part = jnp.einsum(
        "kc,pasc->pksa", cosine_table, filtered, preferred_element_type=jnp.float32
    )
    sine_part = jnp.einsum(
        "kc,pasc->pksa", sine_table, filtered, preferred_element_type=jnp.float32
    )
    real_part = cosine_part[0] + sine_part[1]
    imag_part = cosine_part[1] - sine_part[0]
    spectra = jnp.stack([real_part, imag_part]).astype(jnp.bfloat16)
    spectra = spectra.reshape(2, groups, per_group, spectra_local, stations_local)
    turned = exchange(spectra.transpose(1, 0, 2, 3, 4), "stn", 0)
    turned = turned.reshape(groups, 2, blocks, per_owner, spectra_local, stations_local)
    owned = exchange(turned.transpose(2, 1, 3, 4, 0, 5), "blk", 1)
    owned = owned.reshape(blocks, 2, per_owner, spectra_local, stations)
    chosen = (station_order[None, :] == jnp.arange(stations)[:, None]).astype(jnp.bfloat16)
    ordered = jnp.einsum("bpkns,sr->bpknr", owned, chosen, preferred_element_type=jnp.bfloat16)
    swapped = jnp.stack([ordered[:, 1], -ordered[:, 0]], axis=1)
    left_side = jnp.stack([ordered, swapped])
    visibility = jnp.einsum(
        "qbpkna,bpknc->qkac", left_side, ordered, preferred_element_type=jnp.float32
    )
    power = jnp.einsum("bpkna,bpkna->ka", ordered, ordered, preferred_element_type=jnp.float32)
    scale = lax.rsqrt(power + epsilon)
    coherence = (visibility * scale[None, :, :, None] * scale[None, :, None, :]).astype(
        jnp.bfloat16
    )
    rows = stations // blocks
    coherence = coherence.reshape(2, per_owner, blocks, rows, stations).transpose(2, 0, 1, 3, 4)
    placed = exchange(coherence, "blk", 2)
    return placed.transpose(1, 0, 2, 3, 4).reshape(2, per_group, rows, stations)


def solution(mesh):
    placed = (P(None, "stn", "blk"), P(), P())
    return jax.shard_map(
        per_device,
        mesh=mesh,
        in_specs=placed,
        out_specs=P(None, "stn", "blk", None),
        check_vma=False,
    )
```

```python
import functools

import jax
import jax.numpy as jnp
import ml_dtypes
import numpy as np
from jax import lax
from jax.experimental import pallas as pl
from jax.experimental.pallas import tpu as pltpu
from jax.sharding import PartitionSpec as P

epsilon = 1e-06
MESH = pl.DeviceIdType.MESH
F32 = jnp.float32
BF16 = jnp.bfloat16
GROUPS = 64
BLOCKS = 8
TAPS = 8
CHANNELS = 1024
STATIONS = 512
LOCAL = 8
HALF = 16


@functools.cache
def transform_table():
    index = np.arange(CHANNELS, dtype=np.int64)
    angle = (index[:, None] * index[None, :] % CHANNELS) * (2.0 * np.pi / CHANNELS)
    cosine = np.cos(angle).astype(np.float32)
    sine = np.sin(angle).astype(np.float32)
    rows = np.stack(
        [np.concatenate([cosine, sine], axis=1), np.concatenate([-sine, cosine], axis=1)]
    ).astype(ml_dtypes.bfloat16)
    rows = rows.reshape(2, GROUPS, BLOCKS, 2, 2 * CHANNELS).transpose(3, 1, 0, 2, 4)
    return np.ascontiguousarray(rows.reshape(2, CHANNELS * 2 // 2, 2 * CHANNELS))


def dot(a, b):
    return jnp.dot(a, b, preferred_element_type=F32)


def kernel(
    samples_ref, taps_ref, order_ref, table_ref, out_ref,
    frames, table, edge_out, edge_in, lined, filtered,
    sent, got, turned, blocks, lanes, swap, chosen, ordered, crossed, ordered_t, vis, col_scale,
    row_scale, done,
    load_sem, edge_sem, z_send, z_recv, x_send, x_recv, o_send, o_recv, own_sem,
):
    s = lax.axis_index("stn")
    b = lax.axis_index("blk")
    barrier = pltpu.get_barrier_semaphore()

    def greet_group(step, carry):
        pl.semaphore_signal(
            barrier, inc=1, device_id=(lax.rem(s + step, GROUPS), b), device_id_type=MESH
        )
        return carry

    def greet_block(step, carry):
        pl.semaphore_signal(
            barrier, inc=1, device_id=(s, lax.rem(b + step, BLOCKS)), device_id_type=MESH
        )
        return carry

    load_frames = pltpu.make_async_copy(samples_ref, frames, load_sem.at[0])
    load_frames.start()
    load_tables = [
        pltpu.make_async_copy(table_ref.at[c], table.at[c], load_sem.at[1 + c]) for c in range(2)
    ]
    for load in load_tables:
        load.start()
    lax.fori_loop(1, BLOCKS, greet_block, 0)
    lax.fori_loop(1, GROUPS, greet_group, 0)

    load_frames.wait()
    for t in range(TAPS - 1):
        place = (32 - (TAPS - 1) + t) * CHANNELS
        edge_out[t] = jnp.concatenate(
            [frames[p, :, place : place + CHANNELS].astype(F32) for p in range(2)], axis=0
        ).astype(BF16)

    def filter_half(half):
        def one(block, carry):
            column = pl.multiple_of(block * 128, 128)
            taps = [
                jnp.broadcast_to(taps_ref[t : t + 1, pl.ds(column, 128)], (LOCAL, 128))
                for t in range(TAPS)
            ]
            for p in range(2):
                held = []
                for t in range(HALF * half - (TAPS - 1), HALF * half + HALF):
                    if t < 0:
                        value = edge_in[t + TAPS - 1, :, pl.ds(column, 128)].astype(F32)
                        held.append(value[LOCAL * p : LOCAL * (p + 1)])
                    else:
                        place = pl.multiple_of(t * CHANNELS + column, 128)
                        held.append(frames[p, :, pl.ds(place, 128)].astype(F32))
                for t in range(HALF):
                    total = taps[0] * held[t]
                    for j in range(1, TAPS):
                        total = total + taps[j] * held[t + j]
                    lined[p, LOCAL * t : LOCAL * (t + 1), :] = total
            for p in range(2):
                rows = jnp.concatenate(
                    [lined[p, pl.ds(a, HALF, stride=LOCAL), :] for a in range(LOCAL)], axis=0
                )
                place = pl.multiple_of(p * CHANNELS + column, 128)
                filtered[pl.ds(place, 128), 128 * half : 128 * (half + 1)] = rows.T.astype(BF16)
            return carry

        lax.fori_loop(0, CHANNELS // 128, one, 0)

    def send_group(c, half, block):
        def one(step, carry):
            target = block * 16 + lax.rem(lax.rem(s, 16) + step, 16)

            @pl.when(target != s)
            def _():
                pltpu.make_async_remote_copy(
                    src_ref=sent.at[c, half, target],
                    dst_ref=got.at[c, half, s],
                    send_sem=z_send.at[c, half],
                    recv_sem=z_recv.at[c, half],
                    device_id=(target, b),
                    device_id_type=MESH,
                ).start()

            return carry

        lax.fori_loop(0, 16, one, 0)

    def transform(c, halves):
        def one(step, carry):
            block = lax.rem(s // 16 + step, 4)
            rows = table[c, pl.ds(pl.multiple_of(block * 256, 256), 256), :]
            if len(halves) == 2:
                result = dot(rows, filtered[...])
            else:
                result = dot(rows, filtered[:, 128 * halves[0] : 128 * (halves[0] + 1)])
            for i, half in enumerate(halves):
                sent[c, half, pl.ds(block * 16, 16)] = (
                    result[:, 128 * i : 128 * (i + 1)].astype(BF16).reshape(16, 16, 128)
                )
            for half in halves:
                send_group(c, half, block)
            return carry

        lax.fori_loop(0, 4, one, 0)
        for half in halves:
            got[c, half, s] = sent[c, half, s]

    filter_half(1)
    pl.semaphore_wait(barrier, GROUPS - 1 + BLOCKS - 1)

    edge = pltpu.make_async_remote_copy(
        src_ref=edge_out,
        dst_ref=edge_in,
        send_sem=edge_sem.at[0],
        recv_sem=edge_sem.at[1],
        device_id=(s, lax.rem(b + 1, BLOCKS)),
        device_id_type=MESH,
    )

    @pl.when(b < BLOCKS - 1)
    def _():
        edge.start()

    load_tables[0].wait()
    transform(0, (1,))

    @pl.when(b == 0)
    def _():
        edge_in[...] = jnp.zeros_like(edge_in)

    @pl.when(b > 0)
    def _():
        edge.wait_recv()

    filter_half(0)
    transform(0, (0,))
    load_tables[1].wait()
    transform(1, (1, 0))

    row = lax.broadcasted_iota(jnp.int32, (256, 256), 0)
    column = lax.broadcasted_iota(jnp.int32, (256, 256), 1)
    matches = (row // 16 == column % 16) & (row % 16 == column // 16)
    swap[...] = jnp.where(matches, 1.0, 0.0).astype(BF16)
    for i in range(4):
        place = lax.broadcasted_iota(jnp.int32, (128, STATIONS), 0) + 128 * i
        station = (place % GROUPS) * LOCAL + place // GROUPS
        hot = jnp.where(station == order_ref[...], 1.0, 0.0)
        for j in range(4):
            chosen[128 * j : 128 * (j + 1), 128 * i : 128 * (i + 1)] = (
                hot[:, 128 * j : 128 * (j + 1)].T.astype(BF16)
            )

    def turn(c, half):
        others = pl.ds(0, GROUPS - 1)
        pltpu.make_async_copy(
            sent.at[c, half, others], got.at[c, half, others], z_recv.at[c, half]
        ).wait()
        for i in range(4):
            rows = got[c, half, 16 * i : 16 * (i + 1)].reshape(256, 128)
            rows = dot(swap[...], rows).astype(BF16).reshape(16, 16, 128)
            for x in range(16):
                turned[c, half, x % 8, x // 8, 16 * i : 16 * (i + 1), :] = rows[x]

        def one(step, carry):
            target = lax.rem(b + step, BLOCKS)
            pltpu.make_async_remote_copy(
                src_ref=turned.at[c, half, target],
                dst_ref=blocks.at[c, half, b],
                send_sem=x_send.at[c, half],
                recv_sem=x_recv.at[c, half],
                device_id=(s, target),
                device_id_type=MESH,
            ).start()
            return carry

        lax.fori_loop(1, BLOCKS, one, 0)
        blocks[c, half, b] = turned[c, half, b]

    def line_up(c, half):
        others = pl.ds(0, BLOCKS - 1)
        pltpu.make_async_copy(
            turned.at[c, half, others], blocks.at[c, half, others], x_recv.at[c, half]
        ).wait()
        lane = lax.broadcasted_iota(jnp.int32, (16, 128), 1) // 16

        def one(step, carry):
            first = pl.multiple_of(step * 16, 16)
            for p in range(2):
                held = [blocks[c, half, i, p, pl.ds(first, 16), :].astype(F32) for i in range(8)]
                for d in (1, 2, 4):
                    high = lane & d != 0
                    for i in range(8):
                        if i & d == 0:
                            low_part, high_part = held[i], held[i + d]
                            held[i] = jnp.where(
                                high, pltpu.roll(high_part, 16 * d, 1), low_part
                            )
                            held[i + d] = jnp.where(
                                high, high_part, pltpu.roll(low_part, 128 - 16 * d, 1)
                            )
                for i in range(8):
                    place = pl.multiple_of(i * GROUPS + first, 16)
                    column = 256 * p + 128 * half
                    lanes[pl.ds(place, 16), column : column + 128] = held[i].astype(BF16)
            return carry

        lax.fori_loop(0, GROUPS // 16, one, 0)

    def correlate(c):
        def choose(i, carry):
            rows = pl.ds(pl.multiple_of(i * 128, 128), 128)
            value = dot(chosen[rows, :], lanes[...])
            ordered[rows, :] = value.astype(BF16)
            crossed[rows, 0:256] = value[:, 256:512].astype(BF16)
            crossed[rows, 256:512] = (-value[:, 0:256]).astype(BF16)
            for j in range(4):
                ordered_t[128 * j : 128 * (j + 1), rows] = (
                    value[:, 128 * j : 128 * (j + 1)].T.astype(BF16)
                )
            return carry

        lax.fori_loop(0, 4, choose, 0)

        def multiply(i, carry):
            rows = pl.ds(pl.multiple_of(i * 128, 128), 128)
            vis[0, rows, :] = dot(ordered[rows, :], ordered_t[...])
            vis[1, rows, :] = dot(crossed[rows, :], ordered_t[...])
            return carry

        lax.fori_loop(0, 4, multiply, 0)
        same = lax.broadcasted_iota(jnp.int32, (128, 128), 0) == lax.broadcasted_iota(
            jnp.int32, (128, 128), 1
        )
        for i in range(4):
            rows = slice(128 * i, 128 * (i + 1))
            power = jnp.where(same, vis[0, rows, rows], 0.0)
            col_scale[rows, :] = lax.rsqrt(jnp.sum(power, axis=1, keepdims=True) + epsilon)
            row_scale[:, rows] = lax.rsqrt(jnp.sum(power, axis=0, keepdims=True) + epsilon)

        def finish(step, carry):
            target = lax.rem(b + step, BLOCKS)
            rows = pl.ds(pl.multiple_of(target * 64, 64), 64)
            scale = col_scale[rows, :] * row_scale[...]
            for q in range(2):
                done[c, target, q] = (vis[q, rows, :] * scale).astype(BF16)

            @pl.when(step < BLOCKS)
            def _():
                pltpu.make_async_remote_copy(
                    src_ref=done.at[c, target],
                    dst_ref=out_ref.at[:, 2 * b + c],
                    send_sem=o_send.at[c],
                    recv_sem=o_recv.at[c],
                    device_id=(s, target),
                    device_id_type=MESH,
                ).start()

            return carry

        lax.fori_loop(1, BLOCKS + 1, finish, 0)
        pltpu.make_async_copy(done.at[c, b], out_ref.at[:, 2 * b + c], own_sem.at[c]).start()

    for c in range(2):
        turn(c, 1)
        turn(c, 0)
        line_up(c, 1)
        line_up(c, 0)
        correlate(c)

    @pl.when(b < BLOCKS - 1)
    def _():
        edge.wait_send()

    group_others = pl.ds(0, GROUPS - 1)
    block_others = pl.ds(0, BLOCKS - 1)
    for c in range(2):
        for half in range(2):
            pltpu.make_async_copy(
                sent.at[c, half, group_others], got.at[c, half, group_others], z_send.at[c, half]
            ).wait()
            pltpu.make_async_copy(
                turned.at[c, half, block_others],
                blocks.at[c, half, block_others],
                x_send.at[c, half],
            ).wait()
        pltpu.make_async_copy(
            done.at[c, block_others], done.at[c, block_others], o_send.at[c]
        ).wait()
        pltpu.make_async_copy(
            done.at[c, block_others], done.at[c, block_others], o_recv.at[c]
        ).wait()
        pltpu.make_async_copy(done.at[c, b], out_ref.at[:, 2 * b + c], own_sem.at[c]).wait()


def per_device(samples, fir_taps, station_order):
    anywhere = pl.BlockSpec(memory_space=pl.ANY)
    near = pl.BlockSpec(memory_space=pltpu.VMEM)
    table = jnp.asarray(transform_table())
    dma = pltpu.SemaphoreType.DMA
    return pl.pallas_call(
        kernel,
        out_shape=jax.ShapeDtypeStruct((2, 16, 64, STATIONS), BF16),
        in_specs=[anywhere, near, near, anywhere],
        out_specs=anywhere,
        scratch_shapes=[
            pltpu.VMEM(samples.shape, jnp.int32),
            pltpu.VMEM(table.shape, BF16),
            pltpu.VMEM((TAPS - 1, 2 * LOCAL, CHANNELS), BF16),
            pltpu.VMEM((TAPS - 1, 2 * LOCAL, CHANNELS), BF16),
            pltpu.VMEM((2, 128, 128), F32),
            pltpu.VMEM((2 * CHANNELS, 256), BF16),
            pltpu.VMEM((2, 2, GROUPS, 16, 128), BF16),
            pltpu.VMEM((2, 2, GROUPS, 16, 128), BF16),
            pltpu.VMEM((2, 2, BLOCKS, 2, GROUPS, 128), BF16),
            pltpu.VMEM((2, 2, BLOCKS, 2, GROUPS, 128), BF16),
            pltpu.VMEM((STATIONS, STATIONS), BF16),
            pltpu.VMEM((256, 256), BF16),
            pltpu.VMEM((STATIONS, STATIONS), BF16),
            pltpu.VMEM((STATIONS, STATIONS), BF16),
            pltpu.VMEM((STATIONS, STATIONS), BF16),
            pltpu.VMEM((STATIONS, STATIONS), BF16),
            pltpu.VMEM((2, STATIONS, STATIONS), F32),
            pltpu.VMEM((STATIONS, 1), F32),
            pltpu.VMEM((1, STATIONS), F32),
            pltpu.VMEM((2, BLOCKS, 2, 64, STATIONS), BF16),
            dma((3,)),
            dma((2,)),
            dma((2, 2)),
            dma((2, 2)),
            dma((2, 2)),
            dma((2, 2)),
            dma((2,)),
            dma((2,)),
            dma((2,)),
        ],
        compiler_params=pltpu.CompilerParams(
            collective_id=0, has_side_effects=True, vmem_limit_bytes=48 << 20
        ),
        cost_estimate=pl.CostEstimate(
            flops=4_000_000_000, bytes_accessed=14_000_000, transcendentals=2048
        ),
    )(samples, fir_taps, station_order.reshape(1, STATIONS), table)


def solution(mesh):
    placed = (P(None, "stn", "blk"), P(), P())
    return jax.shard_map(
        per_device,
        mesh=mesh,
        in_specs=placed,
        out_specs=P(None, "stn", "blk", None),
        check_vma=False,
    )
```

```python
import functools

import jax
import jax.numpy as jnp
import ml_dtypes
import numpy as np
from jax import lax
from jax.experimental import pallas as pl
from jax.experimental.pallas import tpu as pltpu
from jax.sharding import PartitionSpec as P

epsilon = 1e-06
MESH = pl.DeviceIdType.MESH
F32 = jnp.float32
BF16 = jnp.bfloat16
GROUPS = 64
BLOCKS = 8
TAPS = 8
CHANNELS = 1024
STATIONS = 512
LOCAL = 8
HALF = 16


@functools.cache
def transform_table():
    index = np.arange(CHANNELS, dtype=np.int64)
    angle = (index[:, None] * index[None, :] % CHANNELS) * (2.0 * np.pi / CHANNELS)
    cosine = np.cos(angle).astype(np.float32)
    sine = np.sin(angle).astype(np.float32)
    rows = np.stack(
        [np.concatenate([cosine, sine], axis=1), np.concatenate([-sine, cosine], axis=1)]
    ).astype(ml_dtypes.bfloat16)
    rows = rows.reshape(2, GROUPS, BLOCKS, 2, 2 * CHANNELS).transpose(3, 1, 0, 2, 4)
    return np.ascontiguousarray(rows.reshape(2, CHANNELS * 2 // 2, 2 * CHANNELS))


def dot(a, b):
    return jnp.dot(a, b, preferred_element_type=F32)


def kernel(
    samples_ref, taps_in, order_in, table_ref, out_ref,
    frames, taps_ref, order_ref, table, edge_out, edge_in, lined, filtered,
    sent, got, turned, blocks, lanes, swap, chosen, pair, ordered_t, power, col_scale,
    row_scale, done, mixed,
    load_sem, edge_sem, z_send, z_recv, x_send, x_recv, o_send, o_recv, own_sem,
):
    s = lax.axis_index("stn")
    b = lax.axis_index("blk")
    barrier = pltpu.get_barrier_semaphore()

    def greet_group(step, carry):
        pl.semaphore_signal(
            barrier, inc=1, device_id=(lax.rem(s + step, GROUPS), b), device_id_type=MESH
        )
        return carry

    def greet_block(step, carry):
        pl.semaphore_signal(
            barrier, inc=1, device_id=(s, lax.rem(b + step, BLOCKS)), device_id_type=MESH
        )
        return carry

    lax.fori_loop(1, GROUPS, greet_group, 0)
    lax.fori_loop(1, BLOCKS, greet_block, 0)
    loads = [
        pltpu.make_async_copy(source, target, load_sem.at[i])
        for i, (source, target) in enumerate(
            [
                (taps_in, taps_ref),
                (samples_ref, frames),
                (table_ref.at[0], table.at[0]),
                (table_ref.at[1], table.at[1]),
                (order_in, order_ref),
            ]
        )
    ]
    for load in loads:
        load.start()
    loads[0].wait()
    loads[1].wait()
    for t in range(TAPS - 1):
        place = (32 - (TAPS - 1) + t) * CHANNELS
        edge_out[t] = jnp.concatenate(
            [frames[p, :, place : place + CHANNELS].astype(F32) for p in range(2)], axis=0
        ).astype(BF16)

    def filter_half(half):
        def one(block, carry):
            column = pl.multiple_of(block * 128, 128)
            taps = [
                jnp.broadcast_to(taps_ref[t : t + 1, pl.ds(column, 128)], (LOCAL, 128))
                for t in range(TAPS)
            ]
            for p in range(2):
                held = []
                for t in range(HALF * half - (TAPS - 1), HALF * half + HALF):
                    if t < 0:
                        value = edge_in[t + TAPS - 1, :, pl.ds(column, 128)].astype(F32)
                        held.append(value[LOCAL * p : LOCAL * (p + 1)])
                    else:
                        place = pl.multiple_of(t * CHANNELS + column, 128)
                        held.append(frames[p, :, pl.ds(place, 128)].astype(F32))
                for t in range(HALF):
                    total = taps[0] * held[t]
                    for j in range(1, TAPS):
                        total = total + taps[j] * held[t + j]
                    lined[p, LOCAL * t : LOCAL * (t + 1), :] = total
            for p in range(2):
                rows = jnp.concatenate(
                    [lined[p, pl.ds(a, HALF, stride=LOCAL), :] for a in range(LOCAL)], axis=0
                )
                place = pl.multiple_of(p * CHANNELS + column, 128)
                filtered[pl.ds(place, 128), 128 * half : 128 * (half + 1)] = rows.T.astype(BF16)
            return carry

        lax.fori_loop(0, CHANNELS // 128, one, 0)

    def send(c, half, target):
        pltpu.make_async_remote_copy(
            src_ref=sent.at[c, half, target],
            dst_ref=got.at[c, half, s],
            send_sem=z_send.at[c, half],
            recv_sem=z_recv.at[c, half],
            device_id=(target, b),
            device_id_type=MESH,
        ).start()

    def send_all(c, half):
        send(c, half, lax.rem(s + GROUPS // 2, GROUPS))

        def one(step, carry):
            offset = GROUPS // 2 - step
            send(c, half, lax.rem(s + offset, GROUPS))
            send(c, half, lax.rem(s + GROUPS - offset, GROUPS))
            return carry

        lax.fori_loop(1, GROUPS // 2, one, 0)

    def transform(c, halves):
        def one(step, carry):
            block = lax.rem(s // 16 + step, 4)
            rows = table[c, pl.ds(pl.multiple_of(block * 256, 256), 256), :]
            if len(halves) == 2:
                result = dot(rows, filtered[...])
            else:
                result = dot(rows, filtered[:, 128 * halves[0] : 128 * (halves[0] + 1)])
            for i, half in enumerate(halves):
                sent[c, half, pl.ds(block * 16, 16)] = (
                    result[:, 128 * i : 128 * (i + 1)].astype(BF16).reshape(16, 16, 128)
                )
            return carry

        lax.fori_loop(0, 4, one, 0)
        for half in halves:
            if (c, half) != (1, 0):
                got[c, half, s] = sent[c, half, s]

    filter_half(1)
    loads[2].wait()
    transform(0, (1,))
    pl.semaphore_wait(barrier, GROUPS - 1 + BLOCKS - 1)

    edge = pltpu.make_async_remote_copy(
        src_ref=edge_out,
        dst_ref=edge_in,
        send_sem=edge_sem.at[0],
        recv_sem=edge_sem.at[1],
        device_id=(s, lax.rem(b + 1, BLOCKS)),
        device_id_type=MESH,
    )

    @pl.when(b < BLOCKS - 1)
    def _():
        edge.start()

    send_all(0, 1)

    @pl.when(b == 0)
    def _():
        edge_in[...] = jnp.zeros_like(edge_in)

    @pl.when(b > 0)
    def _():
        edge.wait_recv()

    filter_half(0)
    transform(0, (0,))
    send_all(0, 0)
    loads[3].wait()
    transform(1, (1, 0))
    loads[4].wait()

    row = lax.broadcasted_iota(jnp.int32, (256, 256), 0)
    column = lax.broadcasted_iota(jnp.int32, (256, 256), 1)
    matches = (row // 16 == column % 16) & (row % 16 == column // 16)
    swap[...] = jnp.where(matches, 1.0, 0.0).astype(BF16)

    def prepare_chosen():
        for i in range(4):
            place = lax.broadcasted_iota(jnp.int32, (128, STATIONS), 0) + 128 * i
            station = (place % GROUPS) * LOCAL + place // GROUPS
            hot = jnp.where(station == order_ref[...], 1.0, 0.0)
            for j in range(4):
                chosen[128 * j : 128 * (j + 1), 128 * i : 128 * (i + 1)] = (
                    hot[:, 128 * j : 128 * (j + 1)].T.astype(BF16)
                )

    def swapped(rows):
        return dot(swap[...], rows.reshape(256, 128)).astype(BF16).reshape(16, 16, 128)

    def arrived(c, half):
        others = pl.ds(0, GROUPS - 1)
        pltpu.make_async_copy(
            got.at[c, half, others], got.at[c, half, others], z_recv.at[c, half]
        ).wait()

    def spread(c, half, source):
        for i in range(4):
            rows = swapped(source[c, half, 16 * i : 16 * (i + 1)])
            for x in range(16):
                turned[c, half, x % 8, x // 8, 16 * i : 16 * (i + 1), :] = rows[x]

        def one(step, carry):
            target = lax.rem(b + step, BLOCKS)
            pltpu.make_async_remote_copy(
                src_ref=turned.at[c, half, target],
                dst_ref=blocks.at[c, half, b],
                send_sem=x_send.at[c, half],
                recv_sem=x_recv.at[c, half],
                device_id=(s, target),
                device_id_type=MESH,
            ).start()
            return carry

        lax.fori_loop(1, BLOCKS, one, 0)
        blocks[c, half, b] = turned[c, half, b]

    def line_up(c, half, ahead=False):
        others = pl.ds(0, BLOCKS - 1)
        pltpu.make_async_copy(
            turned.at[c, half, others], blocks.at[c, half, others], x_recv.at[c, half]
        ).wait()
        lane = lax.broadcasted_iota(jnp.int32, (16, 128), 1) // 16

        def one(step, carry):
            first = pl.multiple_of(step * 16, 16)
            for p in range(2):
                held = [blocks[c, half, i, p, pl.ds(first, 16), :].astype(F32) for i in range(8)]
                for d in (1, 2, 4):
                    high = lane & d != 0
                    for i in range(8):
                        if i & d == 0:
                            low_part, high_part = held[i], held[i + d]
                            held[i] = jnp.where(
                                high, pltpu.roll(high_part, 16 * d, 1), low_part
                            )
                            held[i + d] = jnp.where(
                                high, high_part, pltpu.roll(low_part, 128 - 16 * d, 1)
                            )
                for i in range(8):
                    place = pl.multiple_of(i * GROUPS + first, 16)
                    column = 256 * half + 128 * p
                    if ahead:
                        mixed[8 * p + i, pl.ds(first, 16), :] = held[i].astype(BF16)
                    else:
                        lanes[pl.ds(place, 16), column : column + 128] = held[i].astype(BF16)
            return carry

        lax.fori_loop(0, GROUPS // 16, one, 0)

    def prepare_last():
        line_up(1, 0, ahead=True)
        for i in range(4):
            rows = swapped(mixed[:, 16 * i : 16 * (i + 1), :])
            sent[1, 0, 16 * i : 16 * (i + 1)] = rows
        got[1, 0, s] = sent[1, 0, s]

    def take_last():
        for i in range(4):
            rows = swapped(got[1, 0, 16 * i : 16 * (i + 1)])
            for x in range(16):
                place = x % 8 * GROUPS + 16 * i
                column = 128 * (x // 8)
                lanes[place : place + 16, column : column + 128] = rows[x]

    def choose(half):
        first = 256 * half
        value = dot(chosen[...], lanes[:, first : first + 256])
        pair[0, :, first : first + 256] = value.astype(BF16)
        pair[1, :, first : first + 128] = value[:, 128:256].astype(BF16)
        pair[1, :, first + 128 : first + 256] = (-value[:, 0:128]).astype(BF16)
        for i in range(4):
            total = jnp.zeros((1, 128), F32)
            for j in range(2):
                block = value[128 * i : 128 * (i + 1), 128 * j : 128 * (j + 1)].T
                place = first + 128 * j
                ordered_t[place : place + 128, 128 * i : 128 * (i + 1)] = block.astype(BF16)
                total = total + jnp.sum(block * block, axis=0, keepdims=True)
            power[half : half + 1, 128 * i : 128 * (i + 1)] = total

    def correlate(c):
        scale = lax.rsqrt(power[0:1, :] + power[1:2, :] + epsilon)
        row_scale[...] = scale
        for i in range(4):
            columns = slice(128 * i, 128 * (i + 1))
            col_scale[columns, :] = jnp.broadcast_to(scale[:, columns], (128, 128)).T

        def finish(step, carry):
            block = lax.rem(b // 2 + 1 + step, 4)
            rows = pl.ds(pl.multiple_of(block * 128, 128), 128)
            vis = dot(pair[:, rows, :].reshape(256, STATIONS), ordered_t[...])
            for q in range(2):
                for j in range(4):
                    columns = slice(128 * j, 128 * (j + 1))
                    value = (
                        vis[128 * q : 128 * (q + 1), columns]
                        * col_scale[rows, :]
                        * row_scale[:, columns]
                    ).astype(BF16)
                    for i in range(2):
                        done[c, 2 * block + i, q, :, columns] = value[64 * i : 64 * (i + 1)]
            for i in range(2):
                target = 2 * block + i

                @pl.when(target != b)
                def _():
                    pltpu.make_async_remote_copy(
                        src_ref=done.at[c, target],
                        dst_ref=out_ref.at[:, 2 * b + c],
                        send_sem=o_send.at[c],
                        recv_sem=o_recv.at[c],
                        device_id=(s, target),
                        device_id_type=MESH,
                    ).start()

            return carry

        lax.fori_loop(0, 4, finish, 0)
        pltpu.make_async_copy(done.at[c, b], out_ref.at[:, 2 * b + c], own_sem.at[c]).start()

    spread(1, 0, sent)
    prepare_chosen()
    prepare_last()
    for c in range(2):
        for half in (1, 0):
            arrived(c, half)
            if (c, half) == (1, 0):
                take_last()
            else:
                spread(c, half, got)
                if c == 0:
                    send_all(1, half)
                line_up(c, half)
            choose(half)
        correlate(c)

    @pl.when(b < BLOCKS - 1)
    def _():
        edge.wait_send()

    group_others = pl.ds(0, GROUPS - 1)
    block_others = pl.ds(0, BLOCKS - 1)
    for c in range(2):
        for half in range(2):
            pltpu.make_async_copy(
                sent.at[c, half, group_others], got.at[c, half, group_others], z_send.at[c, half]
            ).wait()
            pltpu.make_async_copy(
                turned.at[c, half, block_others],
                blocks.at[c, half, block_others],
                x_send.at[c, half],
            ).wait()
        pltpu.make_async_copy(
            done.at[c, block_others], done.at[c, block_others], o_send.at[c]
        ).wait()
        pltpu.make_async_copy(
            done.at[c, block_others], done.at[c, block_others], o_recv.at[c]
        ).wait()
        pltpu.make_async_copy(done.at[c, b], out_ref.at[:, 2 * b + c], own_sem.at[c]).wait()


def per_device(samples, fir_taps, station_order):
    anywhere = pl.BlockSpec(memory_space=pl.ANY)
    table = jnp.asarray(transform_table())
    dma = pltpu.SemaphoreType.DMA
    return pl.pallas_call(
        kernel,
        out_shape=jax.ShapeDtypeStruct((2, 16, 64, STATIONS), BF16),
        in_specs=[anywhere] * 4,
        out_specs=anywhere,
        scratch_shapes=[
            pltpu.VMEM(samples.shape, jnp.int32),
            pltpu.VMEM(fir_taps.shape, F32),
            pltpu.VMEM((1, STATIONS), jnp.int32),
            pltpu.VMEM(table.shape, BF16),
            pltpu.VMEM((TAPS - 1, 2 * LOCAL, CHANNELS), BF16),
            pltpu.VMEM((TAPS - 1, 2 * LOCAL, CHANNELS), BF16),
            pltpu.VMEM((2, 128, 128), F32),
            pltpu.VMEM((2 * CHANNELS, 256), BF16),
            pltpu.VMEM((2, 2, GROUPS, 16, 128), BF16),
            pltpu.VMEM((2, 2, GROUPS, 16, 128), BF16),
            pltpu.VMEM((2, 2, BLOCKS, 2, GROUPS, 128), BF16),
            pltpu.VMEM((2, 2, BLOCKS, 2, GROUPS, 128), BF16),
            pltpu.VMEM((STATIONS, STATIONS), BF16),
            pltpu.VMEM((256, 256), BF16),
            pltpu.VMEM((STATIONS, STATIONS), BF16),
            pltpu.VMEM((2, STATIONS, STATIONS), BF16),
            pltpu.VMEM((STATIONS, STATIONS), BF16),
            pltpu.VMEM((2, STATIONS), F32),
            pltpu.VMEM((STATIONS, 128), F32),
            pltpu.VMEM((1, STATIONS), F32),
            pltpu.VMEM((2, BLOCKS, 2, 64, STATIONS), BF16),
            pltpu.VMEM((16, GROUPS, 128), BF16),
            dma((5,)),
            dma((2,)),
            dma((2, 2)),
            dma((2, 2)),
            dma((2, 2)),
            dma((2, 2)),
            dma((2,)),
            dma((2,)),
            dma((2,)),
        ],
        compiler_params=pltpu.CompilerParams(
            collective_id=0, has_side_effects=True, vmem_limit_bytes=61900 << 10
        ),
        cost_estimate=pl.CostEstimate(
            flops=4_000_000_000, bytes_accessed=14_000_000, transcendentals=2048
        ),
    )(samples, fir_taps, station_order.reshape(1, STATIONS), table)


def solution(mesh):
    placed = (P(None, "stn", "blk"), P(), P())
    return jax.shard_map(
        per_device,
        mesh=mesh,
        in_specs=placed,
        out_specs=P(None, "stn", "blk", None),
        check_vma=False,
    )
```

```python
import functools

import jax
import jax.numpy as jnp
import ml_dtypes
import numpy as np
from jax import lax
from jax.experimental import pallas as pl
from jax.experimental.pallas import tpu as pltpu
from jax.sharding import PartitionSpec as P

epsilon = 1e-06
MESH = pl.DeviceIdType.MESH
F32 = jnp.float32
BF16 = jnp.bfloat16
GROUPS = 64
BLOCKS = 8
TAPS = 8
CHANNELS = 1024
STATIONS = 512
LOCAL = 8
HALF = 16


@functools.cache
def transform_table():
    index = np.arange(CHANNELS, dtype=np.int64)
    angle = (index[:, None] * index[None, :] % CHANNELS) * (2.0 * np.pi / CHANNELS)
    cosine = np.cos(angle).astype(np.float32)
    sine = np.sin(angle).astype(np.float32)
    rows = np.stack(
        [np.concatenate([cosine, sine], axis=1), np.concatenate([-sine, cosine], axis=1)]
    ).astype(ml_dtypes.bfloat16)
    rows = rows.reshape(2, GROUPS, BLOCKS, 2, 2 * CHANNELS).transpose(3, 1, 0, 2, 4)
    return np.ascontiguousarray(rows.reshape(2, CHANNELS * 2 // 2, 2 * CHANNELS))


def dot(a, b):
    return jnp.dot(a, b, preferred_element_type=F32)


def kernel(
    samples_ref, taps_in, order_in, table_ref, out_ref,
    frames, taps_ref, order_ref, table, edge_out, edge_in, lined, filtered,
    sent, got, turned, blocks, lanes, swap, chosen, pair, ordered_t, power, col_scale,
    row_scale, done, mixed,
    load_sem, edge_sem, z_send, z_recv, x_send, x_recv, o_send, o_recv, own_sem,
):
    s = lax.axis_index("stn")
    b = lax.axis_index("blk")
    barrier = pltpu.get_barrier_semaphore()

    def greet_group(step, carry):
        pl.semaphore_signal(
            barrier, inc=1, device_id=(lax.rem(s + step, GROUPS), b), device_id_type=MESH
        )
        return carry

    def greet_block(step, carry):
        pl.semaphore_signal(
            barrier, inc=1, device_id=(s, lax.rem(b + step, BLOCKS)), device_id_type=MESH
        )
        return carry

    lax.fori_loop(1, GROUPS, greet_group, 0)
    lax.fori_loop(1, BLOCKS, greet_block, 0)
    loads = [
        pltpu.make_async_copy(source, target, load_sem.at[i])
        for i, (source, target) in enumerate(
            [
                (taps_in, taps_ref),
                (samples_ref, frames),
                (table_ref.at[0], table.at[0]),
                (table_ref.at[1], table.at[1]),
                (order_in, order_ref),
            ]
        )
    ]
    for load in loads:
        load.start()
    loads[0].wait()
    loads[1].wait()
    for t in range(TAPS - 1):
        place = (32 - (TAPS - 1) + t) * CHANNELS
        edge_out[t] = jnp.concatenate(
            [frames[p, :, place : place + CHANNELS].astype(F32) for p in range(2)], axis=0
        ).astype(BF16)

    def filter_half(half):
        def one(block, carry):
            column = pl.multiple_of(block * 128, 128)
            taps = [
                jnp.broadcast_to(taps_ref[t : t + 1, pl.ds(column, 128)], (LOCAL, 128))
                for t in range(TAPS)
            ]
            for p in range(2):
                held = []
                for t in range(HALF * half - (TAPS - 1), HALF * half + HALF):
                    if t < 0:
                        value = edge_in[t + TAPS - 1, :, pl.ds(column, 128)].astype(F32)
                        held.append(value[LOCAL * p : LOCAL * (p + 1)])
                    else:
                        place = pl.multiple_of(t * CHANNELS + column, 128)
                        held.append(frames[p, :, pl.ds(place, 128)].astype(F32))
                for t in range(HALF):
                    total = taps[0] * held[t]
                    for j in range(1, TAPS):
                        total = total + taps[j] * held[t + j]
                    lined[p, LOCAL * t : LOCAL * (t + 1), :] = total
            for p in range(2):
                rows = jnp.concatenate(
                    [lined[p, pl.ds(a, HALF, stride=LOCAL), :] for a in range(LOCAL)], axis=0
                )
                place = pl.multiple_of(p * CHANNELS + column, 128)
                filtered[pl.ds(place, 128), 128 * half : 128 * (half + 1)] = rows.T.astype(BF16)
            return carry

        lax.fori_loop(0, CHANNELS // 128, one, 0)

    def send(c, half, target):
        pltpu.make_async_remote_copy(
            src_ref=sent.at[c, half, target],
            dst_ref=got.at[c, half, s],
            send_sem=z_send.at[c, half],
            recv_sem=z_recv.at[c, half],
            device_id=(target, b),
            device_id_type=MESH,
        ).start()

    def send_all(c, half):
        send(c, half, lax.rem(s + GROUPS // 2, GROUPS))

        def one(step, carry):
            offset = GROUPS // 2 - step
            send(c, half, lax.rem(s + offset, GROUPS))
            send(c, half, lax.rem(s + GROUPS - offset, GROUPS))
            return carry

        lax.fori_loop(1, GROUPS // 2, one, 0)

    def send_last():
        def early(step, carry):
            place = lax.rem(s + step, 16)
            target = place // 8 * 32 + lax.rem(place, 8)

            @pl.when(target != s)
            def _():
                send(1, 0, target)

            return carry

        def late(step, carry):
            offset = GROUPS // 2 - (step + 1) // 2
            target = lax.rem(s + GROUPS + offset * (1 - 2 * lax.rem(step, 2)), GROUPS)

            @pl.when(lax.rem(target, 32) >= 8)
            def _():
                send(1, 0, target)

            return carry

        lax.fori_loop(0, 16, early, 0)
        lax.fori_loop(0, GROUPS - 1, late, 0)

    def transform(c, halves):
        def one(step, carry):
            block = lax.rem(s // 16 + step, 4)
            rows = table[c, pl.ds(pl.multiple_of(block * 256, 256), 256), :]
            if len(halves) == 2:
                result = dot(rows, filtered[...])
            else:
                result = dot(rows, filtered[:, 128 * halves[0] : 128 * (halves[0] + 1)])
            for i, half in enumerate(halves):
                sent[c, half, pl.ds(block * 16, 16)] = (
                    result[:, 128 * i : 128 * (i + 1)].astype(BF16).reshape(16, 16, 128)
                )
            return carry

        lax.fori_loop(0, 4, one, 0)
        for half in halves:
            if (c, half) != (1, 0):
                got[c, half, s] = sent[c, half, s]

    filter_half(1)
    loads[2].wait()
    transform(0, (1,))
    pl.semaphore_wait(barrier, GROUPS - 1 + BLOCKS - 1)

    edge = pltpu.make_async_remote_copy(
        src_ref=edge_out,
        dst_ref=edge_in,
        send_sem=edge_sem.at[0],
        recv_sem=edge_sem.at[1],
        device_id=(s, lax.rem(b + 1, BLOCKS)),
        device_id_type=MESH,
    )

    @pl.when(b < BLOCKS - 1)
    def _():
        edge.start()

    send_all(0, 1)

    @pl.when(b == 0)
    def _():
        edge_in[...] = jnp.zeros_like(edge_in)

    @pl.when(b > 0)
    def _():
        edge.wait_recv()

    filter_half(0)
    transform(0, (0,))
    send_all(0, 0)
    loads[3].wait()
    transform(1, (1, 0))
    loads[4].wait()

    row = lax.broadcasted_iota(jnp.int32, (256, 256), 0)
    column = lax.broadcasted_iota(jnp.int32, (256, 256), 1)
    matches = (row // 16 == column % 16) & (row % 16 == column // 16)
    swap[...] = jnp.where(matches, 1.0, 0.0).astype(BF16)

    def prepare_chosen():
        for i in range(4):
            place = lax.broadcasted_iota(jnp.int32, (128, STATIONS), 0) + 128 * i
            station = (place % GROUPS) * LOCAL + place // GROUPS
            hot = jnp.where(station == order_ref[...], 1.0, 0.0)
            for j in range(4):
                chosen[128 * j : 128 * (j + 1), 128 * i : 128 * (i + 1)] = (
                    hot[:, 128 * j : 128 * (j + 1)].T.astype(BF16)
                )

    def swapped(rows):
        return dot(swap[...], rows.reshape(256, 128)).astype(BF16).reshape(16, 16, 128)

    def arrived(c, half):
        others = pl.ds(0, GROUPS - 1)
        pltpu.make_async_copy(
            got.at[c, half, others], got.at[c, half, others], z_recv.at[c, half]
        ).wait()

    def spread(c, half, source):
        for i in range(4):
            rows = swapped(source[c, half, 16 * i : 16 * (i + 1)])
            for x in range(16):
                turned[c, half, x % 8, x // 8, 16 * i : 16 * (i + 1), :] = rows[x]

        def one(step, carry):
            target = lax.rem(b + step, BLOCKS)
            pltpu.make_async_remote_copy(
                src_ref=turned.at[c, half, target],
                dst_ref=blocks.at[c, half, b],
                send_sem=x_send.at[c, half],
                recv_sem=x_recv.at[c, half],
                device_id=(s, target),
                device_id_type=MESH,
            ).start()
            return carry

        lax.fori_loop(1, BLOCKS, one, 0)
        blocks[c, half, b] = turned[c, half, b]

    def line_up(c, half, ahead=False):
        others = pl.ds(0, BLOCKS - 1)
        pltpu.make_async_copy(
            turned.at[c, half, others], blocks.at[c, half, others], x_recv.at[c, half]
        ).wait()
        lane = lax.broadcasted_iota(jnp.int32, (16, 128), 1) // 16

        def one(step, carry):
            first = pl.multiple_of(step * 16, 16)
            for p in range(2):
                held = [blocks[c, half, i, p, pl.ds(first, 16), :].astype(F32) for i in range(8)]
                for d in (1, 2, 4):
                    high = lane & d != 0
                    for i in range(8):
                        if i & d == 0:
                            low_part, high_part = held[i], held[i + d]
                            held[i] = jnp.where(
                                high, pltpu.roll(high_part, 16 * d, 1), low_part
                            )
                            held[i + d] = jnp.where(
                                high, high_part, pltpu.roll(low_part, 128 - 16 * d, 1)
                            )
                for i in range(8):
                    place = pl.multiple_of(i * GROUPS + first, 16)
                    column = 256 * half + 128 * p
                    if ahead:
                        mixed[8 * p + i, pl.ds(first, 16), :] = held[i].astype(BF16)
                    else:
                        lanes[pl.ds(place, 16), column : column + 128] = held[i].astype(BF16)
            return carry

        lax.fori_loop(0, GROUPS // 16, one, 0)

    def prepare_last():
        line_up(1, 0, ahead=True)
        for i in range(4):
            rows = swapped(mixed[:, 16 * i : 16 * (i + 1), :])
            sent[1, 0, 16 * i : 16 * (i + 1)] = rows
        got[1, 0, s] = sent[1, 0, s]

    def take_last():
        for i in range(4):
            rows = swapped(got[1, 0, 16 * i : 16 * (i + 1)])
            for x in range(16):
                place = x % 8 * GROUPS + 16 * i
                column = 128 * (x // 8)
                lanes[place : place + 16, column : column + 128] = rows[x]

    def choose(half):
        first = 256 * half
        value = dot(chosen[...], lanes[:, first : first + 256])
        pair[0, :, first : first + 256] = value.astype(BF16)
        pair[1, :, first : first + 128] = value[:, 128:256].astype(BF16)
        pair[1, :, first + 128 : first + 256] = (-value[:, 0:128]).astype(BF16)
        for i in range(4):
            total = jnp.zeros((1, 128), F32)
            for j in range(2):
                block = value[128 * i : 128 * (i + 1), 128 * j : 128 * (j + 1)].T
                place = first + 128 * j
                ordered_t[place : place + 128, 128 * i : 128 * (i + 1)] = block.astype(BF16)
                total = total + jnp.sum(block * block, axis=0, keepdims=True)
            power[half : half + 1, 128 * i : 128 * (i + 1)] = total

    def correlate(c):
        scale = lax.rsqrt(power[0:1, :] + power[1:2, :] + epsilon)
        row_scale[...] = scale
        for i in range(4):
            columns = slice(128 * i, 128 * (i + 1))
            col_scale[columns, :] = jnp.broadcast_to(scale[:, columns], (128, 128)).T

        def finish(step, carry):
            block = lax.rem(b // 2 + 1 + step, 4)
            rows = pl.ds(pl.multiple_of(block * 128, 128), 128)
            vis = dot(pair[:, rows, :].reshape(256, STATIONS), ordered_t[...])
            for q in range(2):
                for j in range(4):
                    columns = slice(128 * j, 128 * (j + 1))
                    value = (
                        vis[128 * q : 128 * (q + 1), columns]
                        * col_scale[rows, :]
                        * row_scale[:, columns]
                    ).astype(BF16)
                    for i in range(2):
                        done[c, 2 * block + i, q, :, columns] = value[64 * i : 64 * (i + 1)]
            for i in range(2):
                target = 2 * block + i

                @pl.when(target != b)
                def _():
                    pltpu.make_async_remote_copy(
                        src_ref=done.at[c, target],
                        dst_ref=out_ref.at[:, 2 * b + c],
                        send_sem=o_send.at[c],
                        recv_sem=o_recv.at[c],
                        device_id=(s, target),
                        device_id_type=MESH,
                    ).start()

            return carry

        lax.fori_loop(0, 4, finish, 0)
        pltpu.make_async_copy(done.at[c, b], out_ref.at[:, 2 * b + c], own_sem.at[c]).start()

    spread(1, 0, sent)
    prepare_chosen()
    prepare_last()
    for c in range(2):
        for half in (1, 0):
            arrived(c, half)
            if (c, half) == (1, 0):
                take_last()
            else:
                spread(c, half, got)
                if c == 0 and half == 1:
                    send_all(1, half)
                elif c == 0:
                    send_last()
                line_up(c, half)
            choose(half)
        correlate(c)

    @pl.when(b < BLOCKS - 1)
    def _():
        edge.wait_send()

    group_others = pl.ds(0, GROUPS - 1)
    block_others = pl.ds(0, BLOCKS - 1)
    for c in range(2):
        for half in range(2):
            pltpu.make_async_copy(
                sent.at[c, half, group_others], got.at[c, half, group_others], z_send.at[c, half]
            ).wait()
            pltpu.make_async_copy(
                turned.at[c, half, block_others],
                blocks.at[c, half, block_others],
                x_send.at[c, half],
            ).wait()
        pltpu.make_async_copy(
            done.at[c, block_others], done.at[c, block_others], o_send.at[c]
        ).wait()
        pltpu.make_async_copy(
            done.at[c, block_others], done.at[c, block_others], o_recv.at[c]
        ).wait()
        pltpu.make_async_copy(done.at[c, b], out_ref.at[:, 2 * b + c], own_sem.at[c]).wait()


def per_device(samples, fir_taps, station_order):
    anywhere = pl.BlockSpec(memory_space=pl.ANY)
    table = jnp.asarray(transform_table())
    dma = pltpu.SemaphoreType.DMA
    return pl.pallas_call(
        kernel,
        out_shape=jax.ShapeDtypeStruct((2, 16, 64, STATIONS), BF16),
        in_specs=[anywhere] * 4,
        out_specs=anywhere,
        scratch_shapes=[
            pltpu.VMEM(samples.shape, jnp.int32),
            pltpu.VMEM(fir_taps.shape, F32),
            pltpu.VMEM((1, STATIONS), jnp.int32),
            pltpu.VMEM(table.shape, BF16),
            pltpu.VMEM((TAPS - 1, 2 * LOCAL, CHANNELS), BF16),
            pltpu.VMEM((TAPS - 1, 2 * LOCAL, CHANNELS), BF16),
            pltpu.VMEM((2, 128, 128), F32),
            pltpu.VMEM((2 * CHANNELS, 256), BF16),
            pltpu.VMEM((2, 2, GROUPS, 16, 128), BF16),
            pltpu.VMEM((2, 2, GROUPS, 16, 128), BF16),
            pltpu.VMEM((2, 2, BLOCKS, 2, GROUPS, 128), BF16),
            pltpu.VMEM((2, 2, BLOCKS, 2, GROUPS, 128), BF16),
            pltpu.VMEM((STATIONS, STATIONS), BF16),
            pltpu.VMEM((256, 256), BF16),
            pltpu.VMEM((STATIONS, STATIONS), BF16),
            pltpu.VMEM((2, STATIONS, STATIONS), BF16),
            pltpu.VMEM((STATIONS, STATIONS), BF16),
            pltpu.VMEM((2, STATIONS), F32),
            pltpu.VMEM((STATIONS, 128), F32),
            pltpu.VMEM((1, STATIONS), F32),
            pltpu.VMEM((2, BLOCKS, 2, 64, STATIONS), BF16),
            pltpu.VMEM((16, GROUPS, 128), BF16),
            dma((5,)),
            dma((2,)),
            dma((2, 2)),
            dma((2, 2)),
            dma((2, 2)),
            dma((2, 2)),
            dma((2,)),
            dma((2,)),
            dma((2,)),
        ],
        compiler_params=pltpu.CompilerParams(
            collective_id=0, has_side_effects=True, vmem_limit_bytes=61900 << 10
        ),
        cost_estimate=pl.CostEstimate(
            flops=4_000_000_000, bytes_accessed=14_000_000, transcendentals=2048
        ),
    )(samples, fir_taps, station_order.reshape(1, STATIONS), table)


def solution(mesh):
    placed = (P(None, "stn", "blk"), P(), P())
    return jax.shard_map(
        per_device,
        mesh=mesh,
        in_specs=placed,
        out_specs=P(None, "stn", "blk", None),
        check_vma=False,
    )
```
